512 devices in a mesh: replica: 32 (over z, x), tensor: 16 (over y, core).
Axes of the slice: x: 4, y: 8, z: 8, core: 2. Of those that a mesh axis runs over, the one named last changes fastest.
Arguments:
- queries: bfloat16 [1024, 8192], P('replica', 'tensor'), may hold values from -64 to 64
- cache_keys: bfloat16 [1024, 16, 128, 128], P('replica', 'tensor'), may hold values from -6 to 6
- cache_values: bfloat16 [1024, 16, 128, 128], P('replica', 'tensor'), may hold values from -6 to 6
- page_table: int32 [1024, 2], P('replica'), may hold values from 0 to 31, as said below
- live_slots: int32 [1024], P('replica'), may hold values from 1 to 256, 163840 in all
- migrations: int32 [256, 2], replicated, may hold values from 0 to 31, as said below
Outputs:
- attention: bfloat16 [1024, 8192], P('replica', 'tensor')
- moved_keys: bfloat16 [992, 16, 1, 128, 128], P('replica', 'tensor')
- moved_values: bfloat16 [992, 16, 1, 128, 128], P('replica', 'tensor')
The draws below stay inside these ranges and needn't reach their ends.
Inputs may be any that keep to these rules, and one draw needn't show every extreme that they name: For each replica and each parity p, the entries of page_table at page positions of parity p name distinct pool pages of that replica. `migrations`: rows are grouped by source replica, 8 rows each, in the order of replicas. The sessions of one source are distinct; no destination is its source; at most 1 row of one source name the same destination, and some reach it; each replica is named by at most 31 rows, and some replica by exactly 31.
All inputs are finite; a program needn't handle non-finite values. No bound on the sum of `live_slots` on one device may be relied on, other than what follows from the above.
Results may differ from the reference program's by a relative error of at most 0.0085.
Values may be sent and summed in bfloat16 or wider, within the bound.
No kernel may reach another device: no remote copies, remote signals or barrier semaphores. Data moves between devices by JAX's collectives and lax.ppermute only.
A program may use at most 64 MiB of HBM per device.

```python
import math
import jax
import jax.numpy as jnp
import numpy as np
from jax import lax

HD = 128
GROUP = 8
PAGE = 128
PPS = 2
SESS = 32
OUT = 8
KVH = 8
HEADS = 64
PH = 1
CTX = 256
POOL = 32
IN_MAX = 31
N_REPLICA = 32


def draw_cache_keys(key, part):
    key = jax.random.fold_in(key, 11)
    noise = jax.random.normal(key, (N_REPLICA * POOL, 2 * KVH, PAGE, HD), jnp.float32)
    values = noise
    return jnp.clip(values, -6.0, 6.0).astype(jnp.bfloat16)


def draw_queries(key, part):
    key = jax.random.fold_in(key, 13)
    noise = jax.random.normal(key, (N_REPLICA * SESS, KVH, GROUP, HD), jnp.float32)
    values = jnp.clip(noise, -6.0, 6.0)
    return values.reshape(N_REPLICA * SESS, KVH * GROUP * HD).astype(jnp.bfloat16)


def draw_page_table(key, part):
    key = jax.random.fold_in(key, 17)
    keys = jax.random.split(key, N_REPLICA * 2)
    perms = jax.vmap(lambda sub_key: jax.random.permutation(sub_key, POOL))(keys)
    perms = perms.reshape(N_REPLICA, 2, SESS, PH)
    perms = jnp.transpose(perms, (0, 2, 3, 1))
    return perms.reshape(N_REPLICA * SESS, PPS).astype(jnp.int32)


def draw_migrations(key, part):
    key = jax.random.fold_in(key, 23)
    cold_count = N_REPLICA - OUT - 1
    rows = jnp.arange(N_REPLICA, dtype=jnp.int32)[:, None]
    steps = jnp.arange(OUT, dtype=jnp.int32)[None, :]
    hot_rows = (rows + 1 + steps) % (OUT + 1)
    cold_rows = jnp.where(steps < OUT - 1, steps, OUT + 1 + (rows - OUT) % cold_count)
    virtual = jnp.where(rows <= OUT, hot_rows, cold_rows).astype(jnp.int32)
    row_keys = jax.random.split(jax.random.fold_in(key, 1), N_REPLICA)
    order = jax.vmap(lambda sub_key: jax.random.permutation(sub_key, OUT))(row_keys)
    virtual = jnp.take_along_axis(virtual, order, axis=1)
    sigma = jax.random.permutation(jax.random.fold_in(key, 2), N_REPLICA).astype(jnp.int32)
    physical = sigma[virtual]
    inverse = jnp.argsort(sigma, stable=True)
    dests = physical[inverse]
    sess_keys = jax.random.split(jax.random.fold_in(key, 3), N_REPLICA)
    chosen = jax.vmap(lambda sub_key: jax.random.permutation(sub_key, SESS)[:OUT])(sess_keys)
    return jnp.stack([chosen.reshape(-1), dests.reshape(-1)], axis=1).astype(jnp.int32)


def level_of(key, extent, shards, smallest, top_value):
    factor_of, own = 1.0, jax.random.fold_in(key, 6)
    for dim, blocks in shards:
        draws = jnp.exp(jax.random.uniform(jax.random.fold_in(own, dim), (blocks,), jnp.float32, smallest / len(shards), top_value / len(shards)))
        factor_of = factor_of * jnp.repeat(draws, extent[dim] // blocks).reshape([-1 if axis == dim else 1 for axis in range(len(extent))])
    return factor_of


def profile(count, total, bound, lean):
    portions = [(1 << 20) // math.isqrt(standing ** lean) + 1 for standing in range(2, count + 1)]
    rest, given = total - bound - (count - 1), [1] * (count - 1)
    while rest > 0:
        free = [i for i in range(count - 1) if given[i] < bound]
        whole, left = sum([portions[i] for i in free]), rest
        for i in free:
            addition = min(bound - given[i], max(1, left * portions[i] // whole), rest)
            given[i] = given[i] + addition
            rest = rest - addition
    return np.array([bound] + given)


def ragged(own_key, count, total, reach, slope):
    if count == 2:
        one = jax.random.randint(own_key, (), max(1, total - reach), min(reach, total - 1) + 1)
        return jnp.stack([one, total - one])
    sizes = jnp.asarray(profile(count, total, reach, slope), jnp.int32)
    couples = (count - 1) // 2
    donor, sink = sizes[1:1 + 2 * couples:2], sizes[2:2 + 2 * couples:2]
    slack = jnp.minimum(donor - 1, reach - sink)
    shifted = jax.random.randint(jax.random.fold_in(own_key, 1), (couples,), 0, 1 << 20) % (slack + 1)
    sizes = sizes.at[1:1 + 2 * couples:2].set(donor - shifted).at[2:2 + 2 * couples:2].set(sink + shifted)
    return sizes[jax.random.permutation(jax.random.fold_in(own_key, 2), count)]


def normal_values(stream_key, dims, width, reach, cuts=(), kind=jnp.bfloat16):
    gain = level_of(stream_key, dims, cuts, -0.22, 0.18) if cuts else 1.0
    entries = jax.random.normal(stream_key, dims, jnp.float32) * width * gain
    return jnp.minimum(jnp.maximum(entries, -reach), reach).astype(kind)


def setup_inputs(seed: int = 0) -> dict:
    arg_keys = jax.random.split(jax.random.key(seed), 7)
    queries = draw_queries(jax.random.fold_in(arg_keys[6], 71), 0)
    cache_keys = draw_cache_keys(jax.random.fold_in(arg_keys[6], 71), 0)
    cache_values = normal_values(arg_keys[2], (N_REPLICA * POOL, 2 * KVH, PAGE, HD), 1.0, 6.0, ((0, 32), (1, 16)))
    page_table = draw_page_table(jax.random.fold_in(arg_keys[6], 71), 0)
    live_slots = ragged(arg_keys[4], N_REPLICA * SESS, N_REPLICA * SESS * CTX * 5 // 8, CTX, 2).astype(jnp.int32)
    migrations = draw_migrations(jax.random.fold_in(arg_keys[6], 71), 0)
    return dict(queries=queries, cache_keys=cache_keys, cache_values=cache_values, page_table=page_table, live_slots=live_slots, migrations=migrations)


def per_replica(inputs):
    keys_pool, values_pool, replica_queries, replica_table, replica_live = inputs
    parity = jnp.arange(PPS, dtype=jnp.int32) % 2
    channel = 2 * jnp.arange(KVH, dtype=jnp.int32)[None, :] + parity[:, None]
    keys_sel = keys_pool[replica_table[:, :, None], channel[None, :, :]]
    values_sel = values_pool[replica_table[:, :, None], channel[None, :, :]]
    keys_sel = jnp.transpose(keys_sel, (0, 2, 1, 3, 4)).reshape(SESS, KVH, PPS * PAGE, HD)
    values_sel = jnp.transpose(values_sel, (0, 2, 1, 3, 4)).reshape(SESS, KVH, PPS * PAGE, HD)
    group_queries = replica_queries.reshape(SESS, KVH, GROUP, HD).astype(jnp.float32)
    scores = jnp.einsum('sgqd,sgcd->sgqc', group_queries, keys_sel.astype(jnp.float32)) * (1.0 / math.sqrt(HD))
    live_mask = jnp.arange(PPS * PAGE, dtype=jnp.int32)[None, :] < replica_live[:, None]
    masked = jnp.where(live_mask[:, None, None, :], scores, -jnp.inf)
    peak = lax.optimization_barrier(jnp.max(masked, axis=-1, keepdims=True))
    weights = jnp.exp(masked - peak)
    weights = weights / lax.optimization_barrier(jnp.sum(weights, axis=-1, keepdims=True))
    attended = jnp.einsum('sgqc,sgcd->sgqd', weights, values_sel.astype(jnp.float32))
    return attended.reshape(SESS, KVH * GROUP * HD).astype(jnp.bfloat16)

def reference(queries, cache_keys, cache_values, page_table, live_slots, migrations):
    attention = lax.map(per_replica, (cache_keys.reshape(N_REPLICA, POOL, 2 * KVH, PAGE, HD), cache_values.reshape(N_REPLICA, POOL, 2 * KVH, PAGE, HD), queries.reshape(N_REPLICA, SESS, HEADS * HD), page_table.reshape(N_REPLICA, SESS, PPS), live_slots.reshape(N_REPLICA, SESS)))
    attention = attention.reshape(N_REPLICA * SESS, HEADS * HD)
    row_ids = jnp.arange(N_REPLICA * OUT, dtype=jnp.int32)
    sess_ids = migrations[:, 0].astype(jnp.int32)
    dest_ids = migrations[:, 1].astype(jnp.int32)
    source_ids = row_ids // OUT
    earlier = row_ids[None, :] < row_ids[:, None]
    arrival = lax.optimization_barrier(jnp.sum(earlier & (dest_ids[None, :] == dest_ids[:, None]), axis=1)).astype(jnp.int32)
    table_rows = page_table[source_ids * SESS + sess_ids]
    channel = jnp.arange(2 * KVH, dtype=jnp.int32)
    positions = 2 * jnp.arange(PH, dtype=jnp.int32)[None, :] + (channel % 2)[:, None]
    page_ids = table_rows[:, positions]
    global_rows = source_ids[:, None, None] * POOL + page_ids
    picked_keys = cache_keys[global_rows, channel[None, :, None]]
    picked_values = cache_values[global_rows, channel[None, :, None]]
    target = dest_ids * IN_MAX + arrival
    empty = jnp.zeros((N_REPLICA * IN_MAX, 2 * KVH, PH, PAGE, HD), jnp.bfloat16)
    moved_keys = empty.at[target].set(picked_keys)
    moved_values = empty.at[target].set(picked_values)
    return (attention, moved_keys, moved_values)
```

```python
import math

import jax
import jax.numpy as jnp
from jax import lax
from jax.experimental import pallas as pl
from jax.experimental.pallas import tpu as pltpu
from jax.sharding import PartitionSpec as P

OUT_ROWS = 8
ANY = pl.BlockSpec(memory_space=pl.ANY)
SMEM = pl.BlockSpec(memory_space=pltpu.SMEM)
VMEM = pl.BlockSpec(memory_space=pltpu.VMEM)


def partner(x, axis, bit):
    return lax.ppermute(x, axis, [(i, i ^ 1 << bit) for i in range(lax.axis_size(axis))])


def pack_kernel(table, moves, keys, values, packed, staged, in_sem, out_sem):
    replica, parity = lax.axis_index("replica"), lax.rem(lax.axis_index("tensor"), 2)
    page_len = keys.shape[2]
    loads, stores = [], []
    for j in range(OUT_ROWS):
        row = replica * OUT_ROWS + j
        page = table[parity, moves[0, row]]
        dest = moves[1, row]
        for half, pool in enumerate((keys, values)):
            part = staged.at[j, pl.ds(half * page_len, page_len)]
            loads.append(pltpu.make_async_copy(pool.at[page, 0], part, in_sem.at[2 * j + half]))
            loads[-1].start()
        stores.append(pltpu.make_async_copy(staged.at[j], packed.at[dest], out_sem.at[j]))
    for j, store in enumerate(stores):
        loads[2 * j].wait()
        loads[2 * j + 1].wait()
        store.start()
    for store in stores:
        store.wait()


def attention_kernel(
    table, live, moves, queries, own_k, own_v, other_k, other_v, out, order, qs, acc
):
    replica, parity = lax.axis_index("replica"), lax.rem(lax.axis_index("tensor"), 2)
    sessions, heads, head_dim = qs.shape
    page_len = own_k.shape[2]
    scale = 1.0 / math.sqrt(head_dim)

    def reset(a, carry):
        order[a] = -1
        return carry

    lax.fori_loop(0, order.shape[0], reset, 0)

    def arrive(m, count):
        here = moves[1, m] == replica

        @pl.when(here)
        def _():
            order[count] = m // OUT_ROWS

        return count + here.astype(jnp.int32)

    lax.fori_loop(0, moves.shape[1], arrive, jnp.int32(0))

    for h in range(heads):
        qs[:, h, :] = queries[:, h * head_dim : (h + 1) * head_dim].astype(jnp.float32)
    lane = lax.broadcasted_iota(jnp.int32, (heads, page_len), 1)
    contract_last = (((1,), (1,)), ((), ()))
    contract = (((1,), (0,)), ((), ()))

    def session(s):
        q = qs[s].astype(jnp.bfloat16)
        mine, theirs = table[parity, s], table[1 - parity, s]
        slots = live[s]
        s_own = lax.dot_general(
            q, own_k[mine, 0], contract_last, preferred_element_type=jnp.float32
        )
        s_oth = lax.dot_general(
            q, other_k[theirs, 0], contract_last, preferred_element_type=jnp.float32
        )
        s_own = jnp.where(lane < slots - parity * page_len, s_own * scale, -jnp.inf)
        s_oth = jnp.where(lane < slots - (1 - parity) * page_len, s_oth * scale, -jnp.inf)
        peak = jnp.maximum(
            jnp.max(s_own, axis=1, keepdims=True), jnp.max(s_oth, axis=1, keepdims=True)
        )
        w_own, w_oth = jnp.exp(s_own - peak), jnp.exp(s_oth - peak)
        total = jnp.sum(w_own, axis=1, keepdims=True) + jnp.sum(w_oth, axis=1, keepdims=True)
        o = lax.dot_general(
            w_own.astype(jnp.bfloat16), own_v[mine, 0], contract, preferred_element_type=jnp.float32
        ) + lax.dot_general(
            w_oth.astype(jnp.bfloat16),
            other_v[theirs, 0],
            contract,
            preferred_element_type=jnp.float32,
        )
        acc[s] = o / total

    def block(i, carry):
        for u in range(4):
            session(i * 4 + u)
        return carry

    lax.fori_loop(0, sessions // 4, block, 0)
    for h in range(heads):
        out[:, h * head_dim : (h + 1) * head_dim] = acc[:, h, :].astype(jnp.bfloat16)


def unpack_kernel(order, received, moved_k, moved_v, blank, sem):
    blank[...] = jnp.zeros_like(blank)
    page_len = blank.shape[0]
    slots = moved_k.shape[0]

    def place(a, carry):
        source = order[a]
        for half, moved in enumerate((moved_k, moved_v)):

            @pl.when(source >= 0)
            def _(half=half, moved=moved):
                pltpu.make_async_copy(
                    received.at[source, pl.ds(half * page_len, page_len)],
                    moved.at[a, 0, 0],
                    sem.at[half],
                ).start()

            @pl.when(source < 0)
            def _(half=half, moved=moved):
                pltpu.make_async_copy(blank, moved.at[a, 0, 0], sem.at[half]).start()

        return carry

    lax.fori_loop(0, slots, place, 0)
    for half, moved in enumerate((moved_k, moved_v)):
        pltpu.make_async_copy(moved, moved, sem.at[half]).wait()


def body(queries, cache_keys, cache_values, page_table, live_slots, migrations):
    replicas = lax.axis_size("replica")
    pool, _, page_len, head_dim = cache_keys.shape
    sessions = queries.shape[0]
    heads = queries.shape[1] // head_dim
    table, moves = page_table.T, migrations.T
    row = 2 * page_len
    packed = pl.pallas_call(
        pack_kernel,
        out_shape=jax.ShapeDtypeStruct((replicas, row, head_dim), jnp.bfloat16),
        in_specs=[SMEM, SMEM, ANY, ANY],
        out_specs=ANY,
        scratch_shapes=[
            pltpu.VMEM((OUT_ROWS, row, head_dim), jnp.bfloat16),
            pltpu.SemaphoreType.DMA((2 * OUT_ROWS,)),
            pltpu.SemaphoreType.DMA((OUT_ROWS,)),
        ],
        name="pack",
    )(table, moves, cache_keys, cache_values)
    received = lax.all_to_all(packed, "replica", split_axis=0, concat_axis=0, tiled=True)
    other_keys, other_values = partner((cache_keys, cache_values), "tensor", 0)
    attention, order = pl.pallas_call(
        attention_kernel,
        out_shape=(
            jax.ShapeDtypeStruct(queries.shape, jnp.bfloat16),
            jax.ShapeDtypeStruct((replicas,), jnp.int32),
        ),
        in_specs=[SMEM, SMEM, SMEM, VMEM, VMEM, VMEM, VMEM, VMEM],
        out_specs=(VMEM, SMEM),
        scratch_shapes=[
            pltpu.VMEM((sessions, heads, head_dim), jnp.float32),
            pltpu.VMEM((sessions, heads, head_dim), jnp.float32),
        ],
        compiler_params=pltpu.CompilerParams(vmem_limit_bytes=16 * 1024 * 1024),
        cost_estimate=pl.CostEstimate(
            flops=4 * sessions * heads * row * head_dim,
            bytes_accessed=8 * pool * page_len * head_dim,
            transcendentals=sessions * heads * row,
        ),
        name="attention",
    )(table, live_slots, moves, queries, cache_keys, cache_values, other_keys, other_values)
    moved = jax.ShapeDtypeStruct((replicas - 1, 1, 1, page_len, head_dim), jnp.bfloat16)
    moved_keys, moved_values = pl.pallas_call(
        unpack_kernel,
        out_shape=(moved, moved),
        in_specs=[SMEM, ANY],
        out_specs=(ANY, ANY),
        scratch_shapes=[
            pltpu.VMEM((page_len, head_dim), jnp.bfloat16),
            pltpu.SemaphoreType.DMA((2,)),
        ],
        compiler_params=pltpu.CompilerParams(vmem_limit_bytes=1024 * 1024),
        name="unpack",
    )(order, received)
    return attention, moved_keys, moved_values


def solution(mesh):
    placed = (
        P("replica", "tensor"),
        P("replica", "tensor", None, None),
        P("replica", "tensor", None, None),
        P("replica", None),
        P("replica"),
        P(),
    )
    return jax.shard_map(
        body,
        mesh=mesh,
        in_specs=placed,
        out_specs=(
            P("replica", "tensor"),
            P("replica", "tensor", None, None, None),
            P("replica", "tensor", None, None, None),
        ),
        check_vma=False,
    )
```

```python
import math

import jax
import jax.numpy as jnp
from jax import lax
from jax.experimental import pallas as pl
from jax.experimental.pallas import tpu as pltpu
from jax.sharding import PartitionSpec as P

OUT_ROWS = 8
SEATS = (
    28, 9, 19, 10, 29, 5, 7, 22, 0, 14, 8, 15, 23, 24, 21, 13,
    25, 27, 6, 16, 26, 18, 11, 3, 17, 2, 1, 31, 12, 4, 30, 20,
)
ANY = pl.BlockSpec(memory_space=pl.ANY)
SMEM = pl.BlockSpec(memory_space=pltpu.SMEM)
VMEM = pl.BlockSpec(memory_space=pltpu.VMEM)


def partner(x, axis, bit):
    return lax.ppermute(x, axis, [(i, i ^ 1 << bit) for i in range(lax.axis_size(axis))])


def pack_kernel(
    table_hbm, moves_hbm, seat_hbm, keys, values, packed,
    table, moves, seat, pools, blank, in_sem, out_sem,
):
    replica, parity = lax.axis_index("replica"), lax.rem(lax.axis_index("tensor"), 2)
    page_len = keys.shape[2]
    loads = [
        pltpu.make_async_copy(table_hbm, table, in_sem.at[0]),
        pltpu.make_async_copy(moves_hbm, moves, in_sem.at[1]),
        pltpu.make_async_copy(seat_hbm, seat, in_sem.at[2]),
        pltpu.make_async_copy(keys.at[:, 0], pools.at[0], in_sem.at[3]),
        pltpu.make_async_copy(values.at[:, 0], pools.at[1], in_sem.at[4]),
    ]
    for load in loads:
        load.start()
    blank[...] = jnp.zeros_like(blank)
    for load in loads[:3]:
        load.wait()
    stores = [pltpu.make_async_copy(blank, packed.at[seat[replica]], out_sem.at[2 * OUT_ROWS])]
    stores[0].start()
    rows = []
    for j in range(OUT_ROWS):
        row = replica * OUT_ROWS + j
        rows.append((table[parity, moves[0, row]], seat[moves[1, row]]))
    for half in range(2):
        loads[3 + half].wait()
        for j, (page, dest) in enumerate(rows):
            slot = packed.at[dest, pl.ds(half * page_len, page_len)]
            stores.append(
                pltpu.make_async_copy(pools.at[half, page], slot, out_sem.at[2 * j + half])
            )
            stores[-1].start()
    for store in stores:
        store.wait()


def attention_kernel(
    table, live, moves, seat, queries, own_k, own_v, other_k, other_v, out, order, qs, acc
):
    replica, parity = lax.axis_index("replica"), lax.rem(lax.axis_index("tensor"), 2)
    sessions, heads, head_dim = qs.shape
    page_len = own_k.shape[2]
    scale = 1.0 / math.sqrt(head_dim)

    def reset(a, carry):
        order[a] = seat[replica]
        return carry

    lax.fori_loop(0, order.shape[0], reset, 0)

    def arrive(m, count):
        here = moves[1, m] == replica

        @pl.when(here)
        def _():
            order[count] = seat[m // OUT_ROWS]

        return count + here.astype(jnp.int32)

    lax.fori_loop(0, moves.shape[1], arrive, jnp.int32(0))

    for h in range(heads):
        qs[:, h, :] = queries[:, h * head_dim : (h + 1) * head_dim].astype(jnp.float32)
    lane = lax.broadcasted_iota(jnp.int32, (heads, page_len), 1)
    contract_last = (((1,), (1,)), ((), ()))
    contract = (((1,), (0,)), ((), ()))

    def session(s):
        q = qs[s].astype(jnp.bfloat16)
        mine, theirs = table[parity, s], table[1 - parity, s]
        slots = live[s]
        s_own = lax.dot_general(
            q, own_k[mine, 0], contract_last, preferred_element_type=jnp.float32
        )
        s_oth = lax.dot_general(
            q, other_k[theirs, 0], contract_last, preferred_element_type=jnp.float32
        )
        s_own = jnp.where(lane < slots - parity * page_len, s_own * scale, -jnp.inf)
        s_oth = jnp.where(lane < slots - (1 - parity) * page_len, s_oth * scale, -jnp.inf)
        peak = jnp.maximum(
            jnp.max(s_own, axis=1, keepdims=True), jnp.max(s_oth, axis=1, keepdims=True)
        )
        w_own, w_oth = jnp.exp(s_own - peak), jnp.exp(s_oth - peak)
        total = jnp.sum(w_own, axis=1, keepdims=True) + jnp.sum(w_oth, axis=1, keepdims=True)
        o = lax.dot_general(
            w_own.astype(jnp.bfloat16), own_v[mine, 0], contract, preferred_element_type=jnp.float32
        ) + lax.dot_general(
            w_oth.astype(jnp.bfloat16),
            other_v[theirs, 0],
            contract,
            preferred_element_type=jnp.float32,
        )
        acc[s] = o / total

    def block(i, carry):
        for u in range(4):
            session(i * 4 + u)
        return carry

    lax.fori_loop(0, sessions // 4, block, 0)
    for h in range(heads):
        out[:, h * head_dim : (h + 1) * head_dim] = acc[:, h, :].astype(jnp.bfloat16)


def unpack_kernel(order, received, moved_k, moved_v, sem):
    page_len = moved_k.shape[3]
    for a in range(moved_k.shape[0]):
        source = order[a]
        for half, moved in enumerate((moved_k, moved_v)):
            part = received.at[source, pl.ds(half * page_len, page_len)]
            pltpu.make_async_copy(part, moved.at[a, 0, 0], sem.at[half]).start()
    for half, moved in enumerate((moved_k, moved_v)):
        pltpu.make_async_copy(moved, moved, sem.at[half]).wait()


def body(queries, cache_keys, cache_values, page_table, live_slots, migrations):
    replicas = lax.axis_size("replica")
    pool, _, page_len, head_dim = cache_keys.shape
    sessions = queries.shape[0]
    heads = queries.shape[1] // head_dim
    table, moves = page_table.T, migrations.T
    seat = jnp.asarray([SEATS.index(r) for r in range(replicas)], jnp.int32)
    row = 2 * page_len
    packed = pl.pallas_call(
        pack_kernel,
        out_shape=jax.ShapeDtypeStruct((replicas, row, head_dim), jnp.bfloat16),
        in_specs=[ANY, ANY, ANY, ANY, ANY],
        out_specs=ANY,
        scratch_shapes=[
            pltpu.SMEM(table.shape, jnp.int32),
            pltpu.SMEM(moves.shape, jnp.int32),
            pltpu.SMEM(seat.shape, jnp.int32),
            pltpu.VMEM((2, pool, page_len, head_dim), jnp.bfloat16),
            pltpu.VMEM((row, head_dim), jnp.bfloat16),
            pltpu.SemaphoreType.DMA((5,)),
            pltpu.SemaphoreType.DMA((2 * OUT_ROWS + 1,)),
        ],
        name="pack",
    )(table, moves, seat, cache_keys, cache_values)
    received = lax.all_to_all(
        packed, "replica", split_axis=0, concat_axis=0, axis_index_groups=[list(SEATS)], tiled=True
    )
    other_keys, other_values = partner((cache_keys, cache_values), "tensor", 0)
    attention, order = pl.pallas_call(
        attention_kernel,
        out_shape=(
            jax.ShapeDtypeStruct(queries.shape, jnp.bfloat16),
            jax.ShapeDtypeStruct((replicas,), jnp.int32),
        ),
        in_specs=[SMEM, SMEM, SMEM, SMEM, VMEM, VMEM, VMEM, VMEM, VMEM],
        out_specs=(VMEM, SMEM),
        scratch_shapes=[
            pltpu.VMEM((sessions, heads, head_dim), jnp.float32),
            pltpu.VMEM((sessions, heads, head_dim), jnp.float32),
        ],
        compiler_params=pltpu.CompilerParams(vmem_limit_bytes=16 * 1024 * 1024),
        cost_estimate=pl.CostEstimate(
            flops=4 * sessions * heads * row * head_dim,
            bytes_accessed=8 * pool * page_len * head_dim,
            transcendentals=sessions * heads * row,
        ),
        name="attention",
    )(table, live_slots, moves, seat, queries, cache_keys, cache_values, other_keys, other_values)
    moved = jax.ShapeDtypeStruct((replicas - 1, 1, 1, page_len, head_dim), jnp.bfloat16)
    moved_keys, moved_values = pl.pallas_call(
        unpack_kernel,
        out_shape=(moved, moved),
        in_specs=[SMEM, ANY],
        out_specs=(ANY, ANY),
        scratch_shapes=[pltpu.SemaphoreType.DMA((2,))],
        compiler_params=pltpu.CompilerParams(vmem_limit_bytes=1024 * 1024),
        name="unpack",
    )(order, received)
    return attention, moved_keys, moved_values


def solution(mesh):
    placed = (
        P("replica", "tensor"),
        P("replica", "tensor", None, None),
        P("replica", "tensor", None, None),
        P("replica", None),
        P("replica"),
        P(),
    )
    return jax.shard_map(
        body,
        mesh=mesh,
        in_specs=placed,
        out_specs=(
            P("replica", "tensor"),
            P("replica", "tensor", None, None, None),
            P("replica", "tensor", None, None, None),
        ),
        check_vma=False,
    )
```

```python
import math

import jax
import jax.numpy as jnp
from jax import lax
from jax.experimental import pallas as pl
from jax.experimental.pallas import tpu as pltpu
from jax.sharding import PartitionSpec as P

OUT_ROWS = 8
SEATS = (
    0, 21, 10, 15, 20, 25, 30, 3, 8, 13, 18, 23, 28, 1, 6, 11,
    16, 5, 26, 31, 4, 9, 14, 19, 24, 29, 2, 7, 12, 17, 22, 27,
)
ANY = pl.BlockSpec(memory_space=pl.ANY)
SMEM = pl.BlockSpec(memory_space=pltpu.SMEM)
VMEM = pl.BlockSpec(memory_space=pltpu.VMEM)


def partner(x, axis, bit):
    return lax.ppermute(x, axis, [(i, i ^ 1 << bit) for i in range(lax.axis_size(axis))])


def pack_kernel(
    table_hbm, moves_hbm, seat_hbm, keys, values, packed,
    table, moves, seat, pools, blank, in_sem, out_sem,
):
    replica, parity = lax.axis_index("replica"), lax.rem(lax.axis_index("tensor"), 2)
    page_len = keys.shape[2]
    loads = [
        pltpu.make_async_copy(table_hbm, table, in_sem.at[0]),
        pltpu.make_async_copy(moves_hbm, moves, in_sem.at[1]),
        pltpu.make_async_copy(seat_hbm, seat, in_sem.at[2]),
        pltpu.make_async_copy(keys.at[:, 0], pools.at[0], in_sem.at[3]),
        pltpu.make_async_copy(values.at[:, 0], pools.at[1], in_sem.at[4]),
    ]
    for load in loads:
        load.start()
    blank[...] = jnp.zeros_like(blank)
    for load in loads[:3]:
        load.wait()
    own = packed.at[seat[parity, replica]]
    stores = [pltpu.make_async_copy(blank, own, out_sem.at[2 * OUT_ROWS])]
    stores[0].start()
    rows = []
    for j in range(OUT_ROWS):
        row = replica * OUT_ROWS + j
        rows.append((table[parity, moves[0, row]], seat[parity, moves[1, row]]))
    for half in range(2):
        loads[3 + half].wait()
        for j, (page, dest) in enumerate(rows):
            slot = packed.at[dest, pl.ds(half * page_len, page_len)]
            stores.append(
                pltpu.make_async_copy(pools.at[half, page], slot, out_sem.at[2 * j + half])
            )
            stores[-1].start()
    for store in stores:
        store.wait()


def attention_kernel(
    table, live, moves, seat, queries, own_k, own_v, other_k, other_v, out, order, qs, acc
):
    replica, parity = lax.axis_index("replica"), lax.rem(lax.axis_index("tensor"), 2)
    sessions, heads, head_dim = qs.shape
    page_len = own_k.shape[2]
    scale = 1.0 / math.sqrt(head_dim)

    def reset(a, carry):
        order[a] = seat[parity, replica]
        return carry

    lax.fori_loop(0, order.shape[0], reset, 0)

    def arrive(m, count):
        here = moves[1, m] == replica

        @pl.when(here)
        def _():
            order[count] = seat[parity, m // OUT_ROWS]

        return count + here.astype(jnp.int32)

    lax.fori_loop(0, moves.shape[1], arrive, jnp.int32(0))

    for h in range(heads):
        qs[:, h, :] = queries[:, h * head_dim : (h + 1) * head_dim].astype(jnp.float32)
    lane = lax.broadcasted_iota(jnp.int32, (heads, page_len), 1)
    contract_last = (((1,), (1,)), ((), ()))
    contract = (((1,), (0,)), ((), ()))

    def session(s):
        q = qs[s].astype(jnp.bfloat16)
        mine, theirs = table[parity, s], table[1 - parity, s]
        slots = live[s]
        s_own = lax.dot_general(
            q, own_k[mine, 0], contract_last, preferred_element_type=jnp.float32
        )
        s_oth = lax.dot_general(
            q, other_k[theirs, 0], contract_last, preferred_element_type=jnp.float32
        )
        s_own = jnp.where(lane < slots - parity * page_len, s_own * scale, -jnp.inf)
        s_oth = jnp.where(lane < slots - (1 - parity) * page_len, s_oth * scale, -jnp.inf)
        peak = jnp.maximum(
            jnp.max(s_own, axis=1, keepdims=True), jnp.max(s_oth, axis=1, keepdims=True)
        )
        w_own, w_oth = jnp.exp(s_own - peak), jnp.exp(s_oth - peak)
        total = jnp.sum(w_own, axis=1, keepdims=True) + jnp.sum(w_oth, axis=1, keepdims=True)
        o = lax.dot_general(
            w_own.astype(jnp.bfloat16), own_v[mine, 0], contract, preferred_element_type=jnp.float32
        ) + lax.dot_general(
            w_oth.astype(jnp.bfloat16),
            other_v[theirs, 0],
            contract,
            preferred_element_type=jnp.float32,
        )
        acc[s] = o / total

    def block(i, carry):
        for u in range(4):
            session(i * 4 + u)
        return carry

    lax.fori_loop(0, sessions // 4, block, 0)
    for h in range(heads):
        out[:, h * head_dim : (h + 1) * head_dim] = acc[:, h, :].astype(jnp.bfloat16)


def unpack_kernel(order, received, moved_k, moved_v, sem):
    page_len = moved_k.shape[3]
    for a in range(moved_k.shape[0]):
        source = order[a]
        for half, moved in enumerate((moved_k, moved_v)):
            part = received.at[source, pl.ds(half * page_len, page_len)]
            pltpu.make_async_copy(part, moved.at[a, 0, 0], sem.at[half]).start()
    for half, moved in enumerate((moved_k, moved_v)):
        pltpu.make_async_copy(moved, moved, sem.at[half]).wait()


def body(queries, cache_keys, cache_values, page_table, live_slots, migrations):
    replicas = lax.axis_size("replica")
    pool, _, page_len, head_dim = cache_keys.shape
    sessions = queries.shape[0]
    heads = queries.shape[1] // head_dim
    table, moves = page_table.T, migrations.T
    orders = (SEATS, SEATS[::-1])
    seat = jnp.asarray([[o.index(r) for r in range(replicas)] for o in orders], jnp.int32)
    planes = lax.axis_size("tensor")
    groups = [[r * planes + t for r in orders[t % 2]] for t in range(planes)]
    row = 2 * page_len
    packed = pl.pallas_call(
        pack_kernel,
        out_shape=jax.ShapeDtypeStruct((replicas, row, head_dim), jnp.bfloat16),
        in_specs=[ANY, ANY, ANY, ANY, ANY],
        out_specs=ANY,
        scratch_shapes=[
            pltpu.SMEM(table.shape, jnp.int32),
            pltpu.SMEM(moves.shape, jnp.int32),
            pltpu.SMEM(seat.shape, jnp.int32),
            pltpu.VMEM((2, pool, page_len, head_dim), jnp.bfloat16),
            pltpu.VMEM((row, head_dim), jnp.bfloat16),
            pltpu.SemaphoreType.DMA((5,)),
            pltpu.SemaphoreType.DMA((2 * OUT_ROWS + 1,)),
        ],
        name="pack",
    )(table, moves, seat, cache_keys, cache_values)
    received = lax.all_to_all(
        packed,
        ("replica", "tensor"),
        split_axis=0,
        concat_axis=0,
        axis_index_groups=groups,
        tiled=True,
    )
    other_keys, other_values = partner((cache_keys, cache_values), "tensor", 0)
    attention, order = pl.pallas_call(
        attention_kernel,
        out_shape=(
            jax.ShapeDtypeStruct(queries.shape, jnp.bfloat16),
            jax.ShapeDtypeStruct((replicas,), jnp.int32),
        ),
        in_specs=[SMEM, SMEM, SMEM, SMEM, VMEM, VMEM, VMEM, VMEM, VMEM],
        out_specs=(VMEM, SMEM),
        scratch_shapes=[
            pltpu.VMEM((sessions, heads, head_dim), jnp.float32),
            pltpu.VMEM((sessions, heads, head_dim), jnp.float32),
        ],
        compiler_params=pltpu.CompilerParams(vmem_limit_bytes=16 * 1024 * 1024),
        cost_estimate=pl.CostEstimate(
            flops=4 * sessions * heads * row * head_dim,
            bytes_accessed=8 * pool * page_len * head_dim,
            transcendentals=sessions * heads * row,
        ),
        name="attention",
    )(table, live_slots, moves, seat, queries, cache_keys, cache_values, other_keys, other_values)
    moved = jax.ShapeDtypeStruct((replicas - 1, 1, 1, page_len, head_dim), jnp.bfloat16)
    moved_keys, moved_values = pl.pallas_call(
        unpack_kernel,
        out_shape=(moved, moved),
        in_specs=[SMEM, ANY],
        out_specs=(ANY, ANY),
        scratch_shapes=[pltpu.SemaphoreType.DMA((2,))],
        compiler_params=pltpu.CompilerParams(vmem_limit_bytes=1024 * 1024),
        name="unpack",
    )(order, received)
    return attention, moved_keys, moved_values


def solution(mesh):
    placed = (
        P("replica", "tensor"),
        P("replica", "tensor", None, None),
        P("replica", "tensor", None, None),
        P("replica", None),
        P("replica"),
        P(),
    )
    return jax.shard_map(
        body,
        mesh=mesh,
        in_specs=placed,
        out_specs=(
            P("replica", "tensor"),
            P("replica", "tensor", None, None, None),
            P("replica", "tensor", None, None, None),
        ),
        check_vma=False,
    )
```

```python
import math

import jax
import jax.numpy as jnp
from jax import lax
from jax.experimental import pallas as pl
from jax.experimental.pallas import tpu as pltpu
from jax.sharding import PartitionSpec as P

OUT_ROWS = 8
SEATS = (
    0, 21, 10, 15, 20, 25, 30, 3, 8, 13, 18, 23, 28, 1, 6, 11,
    16, 5, 26, 31, 4, 9, 14, 19, 24, 29, 2, 7, 12, 17, 22, 27,
)
ANY = pl.BlockSpec(memory_space=pl.ANY)
SMEM = pl.BlockSpec(memory_space=pltpu.SMEM)
VMEM = pl.BlockSpec(memory_space=pltpu.VMEM)


def partner(x, axis, bit):
    return lax.ppermute(x, axis, [(i, i ^ 1 << bit) for i in range(lax.axis_size(axis))])


def pack_kernel(
    table_hbm, moves_hbm, seat_hbm, keys, values, packed,
    table, moves, seat, pools, blank, in_sem, out_sem,
):
    replica, parity = lax.axis_index("replica"), lax.rem(lax.axis_index("tensor"), 2)
    page_len = keys.shape[2]
    loads = [
        pltpu.make_async_copy(table_hbm, table, in_sem.at[0]),
        pltpu.make_async_copy(moves_hbm, moves, in_sem.at[1]),
        pltpu.make_async_copy(seat_hbm, seat, in_sem.at[2]),
        pltpu.make_async_copy(keys.at[:, 0], pools.at[0], in_sem.at[3]),
        pltpu.make_async_copy(values.at[:, 0], pools.at[1], in_sem.at[4]),
    ]
    for load in loads:
        load.start()
    blank[...] = jnp.zeros_like(blank)
    for load in loads[:3]:
        load.wait()
    own = packed.at[seat[parity, replica]]
    stores = [pltpu.make_async_copy(blank, own, out_sem.at[2 * OUT_ROWS])]
    stores[0].start()
    rows = []
    for j in range(OUT_ROWS):
        row = replica * OUT_ROWS + j
        rows.append((table[parity, moves[0, row]], seat[parity, moves[1, row]]))
    for half in range(2):
        loads[3 + half].wait()
        for j, (page, dest) in enumerate(rows):
            slot = packed.at[dest, pl.ds(half * page_len, page_len)]
            stores.append(
                pltpu.make_async_copy(pools.at[half, page], slot, out_sem.at[2 * j + half])
            )
            stores[-1].start()
    for store in stores:
        store.wait()


def partial_kernel(
    table, live, moves, seat, queries, other_queries, keys, values, mine, theirs, order, qs
):
    replica, parity = lax.axis_index("replica"), lax.rem(lax.axis_index("tensor"), 2)
    sessions, both, head_dim = qs.shape
    heads = both // 2
    page_len = keys.shape[2]
    scale = 1.0 / math.sqrt(head_dim)

    def reset(a, carry):
        order[a] = seat[parity, replica]
        return carry

    lax.fori_loop(0, order.shape[0], reset, 0)

    def arrive(m, count):
        here = moves[1, m] == replica

        @pl.when(here)
        def _():
            order[count] = seat[parity, m // OUT_ROWS]

        return count + here.astype(jnp.int32)

    lax.fori_loop(0, moves.shape[1], arrive, jnp.int32(0))

    for h in range(heads):
        part = slice(h * head_dim, (h + 1) * head_dim)
        qs[:, h, :] = queries[:, part].astype(jnp.float32)
        qs[:, heads + h, :] = other_queries[:, part].astype(jnp.float32)
    lane = lax.broadcasted_iota(jnp.int32, (both, page_len), 1)

    def session(s):
        page = table[parity, s]
        scores = lax.dot_general(
            qs[s].astype(jnp.bfloat16),
            keys[page, 0],
            (((1,), (1,)), ((), ())),
            preferred_element_type=jnp.float32,
        )
        scores = jnp.where(lane < live[s] - parity * page_len, scores * scale, -jnp.inf)
        peak = jnp.maximum(jnp.max(scores, axis=1, keepdims=True), -1e30)
        weights = jnp.exp(scores - peak)
        total = jnp.sum(weights, axis=1, keepdims=True)
        o = lax.dot_general(
            weights.astype(jnp.bfloat16),
            values[page, 0],
            (((1,), (0,)), ((), ())),
            preferred_element_type=jnp.float32,
        )
        peak = jnp.broadcast_to(peak, o.shape)
        total = jnp.broadcast_to(total, o.shape)
        for part, to in ((slice(0, heads), mine), (slice(heads, both), theirs)):
            to[0, s], to[1, s], to[2, s] = o[part], peak[part], total[part]

    def block(i, carry):
        for u in range(4):
            session(i * 4 + u)
        return carry

    lax.fori_loop(0, sessions // 4, block, 0)


def combine_kernel(mine, theirs, out):
    heads, head_dim = mine.shape[2:]
    for h in range(heads):
        o1, m1, l1 = (mine[i, :, h, :] for i in range(3))
        o2, m2, l2 = (theirs[i, :, h, :] for i in range(3))
        peak = jnp.maximum(m1, m2)
        w1, w2 = jnp.exp(m1 - peak), jnp.exp(m2 - peak)
        o = (o1 * w1 + o2 * w2) / (l1 * w1 + l2 * w2)
        out[:, h * head_dim : (h + 1) * head_dim] = o.astype(jnp.bfloat16)


def unpack_kernel(order, received, moved_k, moved_v, sem):
    page_len = moved_k.shape[3]
    for a in range(moved_k.shape[0]):
        source = order[a]
        for half, moved in enumerate((moved_k, moved_v)):
            part = received.at[source, pl.ds(half * page_len, page_len)]
            pltpu.make_async_copy(part, moved.at[a, 0, 0], sem.at[half]).start()
    for half, moved in enumerate((moved_k, moved_v)):
        pltpu.make_async_copy(moved, moved, sem.at[half]).wait()


def body(queries, cache_keys, cache_values, page_table, live_slots, migrations):
    replicas = lax.axis_size("replica")
    pool, _, page_len, head_dim = cache_keys.shape
    sessions = queries.shape[0]
    heads = queries.shape[1] // head_dim
    table, moves = page_table.T, migrations.T
    orders = (SEATS, SEATS[::-1])
    seat = jnp.asarray([[o.index(r) for r in range(replicas)] for o in orders], jnp.int32)
    planes = lax.axis_size("tensor")
    groups = [[r * planes + t for r in orders[t % 2]] for t in range(planes)]
    row = 2 * page_len
    packed = pl.pallas_call(
        pack_kernel,
        out_shape=jax.ShapeDtypeStruct((replicas, row, head_dim), jnp.bfloat16),
        in_specs=[ANY, ANY, ANY, ANY, ANY],
        out_specs=ANY,
        scratch_shapes=[
            pltpu.SMEM(table.shape, jnp.int32),
            pltpu.SMEM(moves.shape, jnp.int32),
            pltpu.SMEM(seat.shape, jnp.int32),
            pltpu.VMEM((2, pool, page_len, head_dim), jnp.bfloat16),
            pltpu.VMEM((row, head_dim), jnp.bfloat16),
            pltpu.SemaphoreType.DMA((5,)),
            pltpu.SemaphoreType.DMA((2 * OUT_ROWS + 1,)),
        ],
        name="pack",
    )(table, moves, seat, cache_keys, cache_values)
    received = lax.all_to_all(
        packed,
        ("replica", "tensor"),
        split_axis=0,
        concat_axis=0,
        axis_index_groups=groups,
        tiled=True,
    )
    part = jax.ShapeDtypeStruct((3, sessions, heads, head_dim), jnp.float32)
    mine, theirs, order = pl.pallas_call(
        partial_kernel,
        out_shape=(part, part, jax.ShapeDtypeStruct((replicas,), jnp.int32)),
        in_specs=[SMEM, SMEM, SMEM, SMEM, VMEM, VMEM, VMEM, VMEM],
        out_specs=(VMEM, VMEM, SMEM),
        scratch_shapes=[pltpu.VMEM((sessions, 2 * heads, head_dim), jnp.float32)],
        compiler_params=pltpu.CompilerParams(vmem_limit_bytes=16 * 1024 * 1024),
        cost_estimate=pl.CostEstimate(
            flops=4 * sessions * heads * row * head_dim,
            bytes_accessed=4 * pool * page_len * head_dim,
            transcendentals=sessions * heads * row,
        ),
        name="partial",
    )(
        table, live_slots, moves, seat, queries, partner(queries, "tensor", 0),
        cache_keys, cache_values,
    )
    attention = pl.pallas_call(
        combine_kernel,
        out_shape=jax.ShapeDtypeStruct(queries.shape, jnp.bfloat16),
        in_specs=[VMEM, VMEM],
        out_specs=VMEM,
        compiler_params=pltpu.CompilerParams(vmem_limit_bytes=16 * 1024 * 1024),
        name="combine",
    )(mine, partner(theirs, "tensor", 0))
    moved = jax.ShapeDtypeStruct((replicas - 1, 1, 1, page_len, head_dim), jnp.bfloat16)
    moved_keys, moved_values = pl.pallas_call(
        unpack_kernel,
        out_shape=(moved, moved),
        in_specs=[SMEM, ANY],
        out_specs=(ANY, ANY),
        scratch_shapes=[pltpu.SemaphoreType.DMA((2,))],
        compiler_params=pltpu.CompilerParams(vmem_limit_bytes=1024 * 1024),
        name="unpack",
    )(order, received)
    return attention, moved_keys, moved_values


def solution(mesh):
    placed = (
        P("replica", "tensor"),
        P("replica", "tensor", None, None),
        P("replica", "tensor", None, None),
        P("replica", None),
        P("replica"),
        P(),
    )
    return jax.shard_map(
        body,
        mesh=mesh,
        in_specs=placed,
        out_specs=(
            P("replica", "tensor"),
            P("replica", "tensor", None, None, None),
            P("replica", "tensor", None, None, None),
        ),
        check_vma=False,
    )
```

```python
import math

import jax
import jax.numpy as jnp
from jax import lax
from jax.experimental import pallas as pl
from jax.experimental.pallas import tpu as pltpu
from jax.sharding import PartitionSpec as P

OUT_ROWS = 8
SEATS = (
    (
        0, 21, 10, 15, 20, 25, 30, 3, 8, 13, 18, 23, 28, 1, 6, 11,
        16, 5, 26, 31, 4, 9, 14, 19, 24, 29, 2, 7, 12, 17, 22, 27,
    ),
    (
        27, 22, 17, 12, 7, 2, 29, 24, 19, 14, 9, 4, 31, 26, 5, 16,
        11, 6, 1, 28, 23, 18, 13, 8, 3, 30, 25, 20, 15, 10, 21, 0,
    ),
)
ANY = pl.BlockSpec(memory_space=pl.ANY)
SMEM = pl.BlockSpec(memory_space=pltpu.SMEM)
VMEM = pl.BlockSpec(memory_space=pltpu.VMEM)


def partner(x, axis, bit):
    return lax.ppermute(x, axis, [(i, i ^ 1 << bit) for i in range(lax.axis_size(axis))])


def pack_kernel(
    table_hbm, moves_hbm, seat_hbm, keys, values, packed,
    table, moves, seat, pools, blank, in_sem, out_sem,
):
    replica, parity = lax.axis_index("replica"), lax.rem(lax.axis_index("tensor"), 2)
    page_len = keys.shape[2]
    loads = [
        pltpu.make_async_copy(table_hbm, table, in_sem.at[0]),
        pltpu.make_async_copy(moves_hbm, moves, in_sem.at[1]),
        pltpu.make_async_copy(seat_hbm, seat, in_sem.at[2]),
        pltpu.make_async_copy(keys.at[:, 0], pools.at[0], in_sem.at[3]),
        pltpu.make_async_copy(values.at[:, 0], pools.at[1], in_sem.at[4]),
    ]
    for load in loads:
        load.start()
    blank[...] = jnp.zeros_like(blank)
    for load in loads[:3]:
        load.wait()
    own = packed.at[seat[parity, replica]]
    stores = [pltpu.make_async_copy(blank, own, out_sem.at[2 * OUT_ROWS])]
    stores[0].start()
    rows = []
    for j in range(OUT_ROWS):
        row = replica * OUT_ROWS + j
        rows.append((table[parity, moves[0, row]], seat[parity, moves[1, row]]))
    for half in range(2):
        loads[3 + half].wait()
        for j, (page, dest) in enumerate(rows):
            slot = packed.at[dest, pl.ds(half * page_len, page_len)]
            stores.append(
                pltpu.make_async_copy(pools.at[half, page], slot, out_sem.at[2 * j + half])
            )
            stores[-1].start()
    for store in stores:
        store.wait()


def attention_kernel(
    table, live, moves, seat, queries, own_k, own_v, other_k, other_v, out, order, qs, acc
):
    replica, parity = lax.axis_index("replica"), lax.rem(lax.axis_index("tensor"), 2)
    sessions, heads, head_dim = qs.shape
    page_len = own_k.shape[2]
    scale = 1.0 / math.sqrt(head_dim)

    def reset(a, carry):
        order[a] = seat[parity, replica]
        return carry

    lax.fori_loop(0, order.shape[0], reset, 0)

    def arrive(m, count):
        here = moves[1, m] == replica

        @pl.when(here)
        def _():
            order[count] = seat[parity, m // OUT_ROWS]

        return count + here.astype(jnp.int32)

    lax.fori_loop(0, moves.shape[1], arrive, jnp.int32(0))

    for h in range(heads):
        qs[:, h, :] = queries[:, h * head_dim : (h + 1) * head_dim].astype(jnp.float32)
    lane = lax.broadcasted_iota(jnp.int32, (heads, page_len), 1)
    contract_last = (((1,), (1,)), ((), ()))
    contract = (((1,), (0,)), ((), ()))

    def session(s):
        q = qs[s].astype(jnp.bfloat16)
        mine, theirs = table[parity, s], table[1 - parity, s]
        slots = live[s]
        s_own = lax.dot_general(
            q, own_k[mine, 0], contract_last, preferred_element_type=jnp.float32
        )
        s_oth = lax.dot_general(
            q, other_k[theirs, 0], contract_last, preferred_element_type=jnp.float32
        )
        s_own = jnp.where(lane < slots - parity * page_len, s_own * scale, -jnp.inf)
        s_oth = jnp.where(lane < slots - (1 - parity) * page_len, s_oth * scale, -jnp.inf)
        peak = jnp.maximum(
            jnp.max(s_own, axis=1, keepdims=True), jnp.max(s_oth, axis=1, keepdims=True)
        )
        w_own, w_oth = jnp.exp(s_own - peak), jnp.exp(s_oth - peak)
        total = jnp.sum(w_own, axis=1, keepdims=True) + jnp.sum(w_oth, axis=1, keepdims=True)
        o = lax.dot_general(
            w_own.astype(jnp.bfloat16), own_v[mine, 0], contract, preferred_element_type=jnp.float32
        ) + lax.dot_general(
            w_oth.astype(jnp.bfloat16),
            other_v[theirs, 0],
            contract,
            preferred_element_type=jnp.float32,
        )
        acc[s] = o / total

    def block(i, carry):
        for u in range(4):
            session(i * 4 + u)
        return carry

    lax.fori_loop(0, sessions // 4, block, 0)
    for h in range(heads):
        out[:, h * head_dim : (h + 1) * head_dim] = acc[:, h, :].astype(jnp.bfloat16)


def unpack_kernel(order, received, moved_k, moved_v, sem):
    page_len = moved_k.shape[3]
    for a in range(moved_k.shape[0]):
        source = order[a]
        for half, moved in enumerate((moved_k, moved_v)):
            part = received.at[source, pl.ds(half * page_len, page_len)]
            pltpu.make_async_copy(part, moved.at[a, 0, 0], sem.at[half]).start()
    for half, moved in enumerate((moved_k, moved_v)):
        pltpu.make_async_copy(moved, moved, sem.at[half]).wait()


def body(queries, cache_keys, cache_values, page_table, live_slots, migrations):
    replicas = lax.axis_size("replica")
    pool, _, page_len, head_dim = cache_keys.shape
    sessions = queries.shape[0]
    heads = queries.shape[1] // head_dim
    table, moves = page_table.T, migrations.T
    seat = jnp.asarray([[o.index(r) for r in range(replicas)] for o in SEATS], jnp.int32)
    planes = lax.axis_size("tensor")
    groups = [[r * planes + t for r in SEATS[t % 2]] for t in range(planes)]
    row = 2 * page_len
    packed = pl.pallas_call(
        pack_kernel,
        out_shape=jax.ShapeDtypeStruct((replicas, row, head_dim), jnp.bfloat16),
        in_specs=[ANY, ANY, ANY, ANY, ANY],
        out_specs=ANY,
        scratch_shapes=[
            pltpu.SMEM(table.shape, jnp.int32),
            pltpu.SMEM(moves.shape, jnp.int32),
            pltpu.SMEM(seat.shape, jnp.int32),
            pltpu.VMEM((2, pool, page_len, head_dim), jnp.bfloat16),
            pltpu.VMEM((row, head_dim), jnp.bfloat16),
            pltpu.SemaphoreType.DMA((5,)),
            pltpu.SemaphoreType.DMA((2 * OUT_ROWS + 1,)),
        ],
        name="pack",
    )(table, moves, seat, cache_keys, cache_values)
    received = lax.all_to_all(
        packed,
        ("replica", "tensor"),
        split_axis=0,
        concat_axis=0,
        axis_index_groups=groups,
        tiled=True,
    )
    other_keys, other_values = partner((cache_keys, cache_values), "tensor", 0)
    attention, order = pl.pallas_call(
        attention_kernel,
        out_shape=(
            jax.ShapeDtypeStruct(queries.shape, jnp.bfloat16),
            jax.ShapeDtypeStruct((replicas,), jnp.int32),
        ),
        in_specs=[SMEM, SMEM, SMEM, SMEM, VMEM, VMEM, VMEM, VMEM, VMEM],
        out_specs=(VMEM, SMEM),
        scratch_shapes=[
            pltpu.VMEM((sessions, heads, head_dim), jnp.float32),
            pltpu.VMEM((sessions, heads, head_dim), jnp.float32),
        ],
        compiler_params=pltpu.CompilerParams(vmem_limit_bytes=16 * 1024 * 1024),
        cost_estimate=pl.CostEstimate(
            flops=4 * sessions * heads * row * head_dim,
            bytes_accessed=8 * pool * page_len * head_dim,
            transcendentals=sessions * heads * row,
        ),
        name="attention",
    )(table, live_slots, moves, seat, queries, cache_keys, cache_values, other_keys, other_values)
    moved = jax.ShapeDtypeStruct((replicas - 1, 1, 1, page_len, head_dim), jnp.bfloat16)
    moved_keys, moved_values = pl.pallas_call(
        unpack_kernel,
        out_shape=(moved, moved),
        in_specs=[SMEM, ANY],
        out_specs=(ANY, ANY),
        scratch_shapes=[pltpu.SemaphoreType.DMA((2,))],
        compiler_params=pltpu.CompilerParams(vmem_limit_bytes=1024 * 1024),
        name="unpack",
    )(order, received)
    return attention, moved_keys, moved_values


def solution(mesh):
    placed = (
        P("replica", "tensor"),
        P("replica", "tensor", None, None),
        P("replica", "tensor", None, None),
        P("replica", None),
        P("replica"),
        P(),
    )
    return jax.shard_map(
        body,
        mesh=mesh,
        in_specs=placed,
        out_specs=(
            P("replica", "tensor"),
            P("replica", "tensor", None, None, None),
            P("replica", "tensor", None, None, None),
        ),
        check_vma=False,
    )
```
